512 devices in a mesh: dp: 64 (over z, y_lo, core), tensor: 8 (over y_hi, x).
Axes of the slice: x: 4, y: 8 (y_hi: 2, y_lo: 4; y = y_hi * 4 + y_lo), z: 8, core: 2. Of those that a mesh axis runs over, the one named last changes fastest.
Arguments:
- hidden_acts: bfloat16 [26624, 28672], P('dp', 'tensor'), may hold values from -6 to 6
- out_grads: bfloat16 [26624, 8192], P('dp', 'tensor'), may hold values from -6 to 6
- left_factors: bfloat16 [64, 28672, 128], P('dp', 'tensor'), may hold values from -0.03125 to 0.03125
- right_factors: bfloat16 [64, 8192, 128], P('dp', 'tensor'), may hold values from -0.0625 to 0.0625
- doc_tokens: int32 [64, 8], P('dp'), may hold values from 1 to 104, 416 in all within a row
- owners: int32 [2], replicated, may hold values from 0 to 63
Outputs:
- scores: float32 [512, 8], P('dp')
The draws below stay inside these ranges and needn't reach their ends.
Inputs may be any that keep to these rules, and one draw needn't show every extreme that they name: `doc_tokens`: each dp index's counts sum to 416; the largest of each row is 104.
All inputs are finite; a program needn't handle non-finite values.
Results may differ from the reference program's by a relative error of at most 0.0003.
Values may be sent and summed in bfloat16 or wider, within the bound.
No kernel may reach another device: no remote copies, remote signals or barrier semaphores. Data moves between devices by JAX's collectives and lax.ppermute only.
A program may use at most 64 MiB of HBM per device.

```python
import math
import jax
import jax.numpy as jnp
import numpy as np
from jax import lax

D = 8192
FF = 28672
TOK_DEV = 416
DOCS_DEV = 8
MOST = 104
QB = 4
RANK = 32
TOKENS = 26624
DOCS = 512
N_DP = 64


def shard_levels(key, dims, pieces, low, high):
    def one(axis_at, shards_of):
        steps = jax.random.uniform(jax.random.fold_in(jax.random.fold_in(key, 6), axis_at), (shards_of,), jnp.float32, low / len(pieces), high / len(pieces))
        return jnp.repeat(jnp.exp(steps), dims[axis_at] // shards_of).reshape((-1,) + (1,) * (len(dims) - axis_at - 1))

    factor_of = one(*pieces[0])
    for cut in pieces[1:]:
        factor_of = factor_of * one(*cut)
    return factor_of


def split_up(count, total, limit, lean):
    portions = [(1 << 20) // math.isqrt(standing ** lean) + 1 for standing in range(2, count + 1)]
    spare, counts = total - limit - (count - 1), [1] * (count - 1)
    while spare > 0:
        candidates = [i for i in range(count - 1) if counts[i] < limit]
        mass, left = sum([portions[i] for i in candidates]), spare
        for i in candidates:
            more = min(limit - counts[i], max(1, left * portions[i] // mass), spare)
            counts[i] = counts[i] + more
            spare = spare - more
    return np.array([limit] + counts)


def ragged(stream_key, count, total, limit, lean):
    if count == 2:
        one = jax.random.randint(stream_key, (), max(1, total - limit), min(limit, total - 1) + 1)
        return jnp.stack([one, total - one])
    lengths = jnp.asarray(split_up(count, total, limit, lean), jnp.int32)
    twos = (count - 1) // 2
    donor, sink = lengths[1:1 + 2 * twos:2], lengths[2:2 + 2 * twos:2]
    margin = jnp.minimum(donor - 1, limit - sink)
    moved = jax.random.randint(jax.random.fold_in(stream_key, 1), (twos,), 0, 1 << 20) % (margin + 1)
    lengths = lengths.at[1:1 + 2 * twos:2].set(donor - moved).at[2:2 + 2 * twos:2].set(sink + moved)
    return lengths[jax.random.permutation(jax.random.fold_in(stream_key, 2), count)]


def bell_draw(own_key, dims, deviation, most, cuts=(), held_as=jnp.bfloat16):
    factor_of = shard_levels(own_key, dims, cuts, -0.22, 0.18) if cuts else 1.0
    drawn = jax.random.normal(own_key, dims, jnp.float32) * deviation * factor_of
    return jnp.minimum(jnp.maximum(drawn, -most), most).astype(held_as)


def setup_inputs(seed: int = 0) -> dict:
    key_of = jax.random.split(jax.random.key(seed), 7)
    return {
        "hidden_acts": bell_draw(key_of[0], (TOKENS, FF), 1.0, 6.0, ((0, 64), (1, 8))),
        "out_grads": bell_draw(key_of[1], (TOKENS, D), 1.0, 6.0, ((0, 64), (1, 8))),
        "left_factors": bell_draw(key_of[2], (N_DP, FF, QB * RANK), FF ** -0.5, 0.03125, ((0, 64), (1, 8))),
        "right_factors": bell_draw(key_of[3], (N_DP, D, QB * RANK), D ** -0.5, 0.0625, ((0, 64), (1, 8))),
        "doc_tokens": jax.vmap(lambda own: ragged(own, DOCS_DEV, TOK_DEV, MOST, 2))(jax.random.split(key_of[4], N_DP)).reshape((N_DP, DOCS_DEV)).astype(jnp.int32),
        "owners": jax.random.randint(key_of[5], (2,), 0, N_DP).astype(jnp.int32),
    }


def doc_masks(doc_tokens):
    ends = jnp.cumsum(doc_tokens, axis=1)
    starts = ends - doc_tokens
    pos = jnp.arange(TOK_DEV, dtype=jnp.int32)
    inside = (pos[None, None, :] >= starts[:, :, None]) & (pos[None, None, :] < ends[:, :, None])
    return inside.astype(jnp.float32)

def reference(hidden_acts, out_grads, left_factors, right_factors, doc_tokens, owners):
    columns = []
    for batch in range(2):
        left_now = left_factors[owners[batch]]
        right_now = right_factors[owners[batch]]
        proj_h = jnp.dot(hidden_acts, left_now, preferred_element_type=jnp.float32)
        proj_g = jnp.dot(out_grads, right_now, preferred_element_type=jnp.float32)
        columns.append((proj_h * proj_g).reshape(TOKENS, QB, RANK).sum(axis=2))
    token_score = jnp.concatenate(columns, axis=1).reshape(N_DP, TOK_DEV, 2 * QB)
    masks = doc_masks(doc_tokens)
    summed = jnp.einsum('dnt,dtc->dnc', masks, token_score, precision=lax.Precision.HIGHEST)
    return (summed / jnp.sqrt(jnp.float32(RANK * MOST))).reshape(DOCS, 2 * QB)
```

```python
import jax
import jax.numpy as jnp
from jax import lax
from jax.sharding import Mesh
from jax.sharding import PartitionSpec as P

QB = 4
RANK = 32
COLS = QB * RANK
Z, Y, C, H, X = 8, 4, 2, 2, 4


def swap(block, axis):
    return lax.ppermute(block, axis, [(0, 1), (1, 0)])


def halves(left, right):
    rows_l, rows_r = left.shape[0] // 2, right.shape[0] // 2
    return jnp.concatenate([left[:rows_l], right[:rows_r], left[rows_l:], right[rows_r:]], axis=0)


def shards(hidden_acts, out_grads, left_factors, right_factors, doc_tokens, owners):
    tok_rows = hidden_acts.shape[0]
    core, hi, at_x = lax.axis_index("c"), lax.axis_index("h"), lax.axis_index("x")
    rows_l, rows_r = left_factors.shape[1] // 2, right_factors.shape[1] // 2

    own = halves(left_factors[0], right_factors[0])
    piece = own.shape[0] // (Z * Y * C)
    got = lax.all_to_all(own, ("c", "z", "y"), 0, 0, tiled=True)
    got = got.reshape(Z * Y * C, piece, COLS)
    picked = []
    for batch in range(2):
        owner = owners[batch]
        source = (owner % C) * (Z * Y) + owner // C
        picked.append(lax.dynamic_index_in_dim(got, source, 0, keepdims=False))
    picked = jnp.concatenate(picked, axis=1)

    copies = jnp.broadcast_to(picked[None], (Z * Y, piece, 2 * COLS)).reshape(Z * Y * piece, 2 * COLS)
    mine = lax.all_to_all(copies, ("z", "y"), 0, 0, tiled=True)
    other = swap(mine, "c")

    def project(part, side):
        acts = lax.dynamic_slice_in_dim(hidden_acts, side * rows_l, rows_l, 1)
        grads = lax.dynamic_slice_in_dim(out_grads, side * rows_r, rows_r, 1)
        return (
            jnp.dot(acts, part[:rows_l], preferred_element_type=jnp.float32),
            jnp.dot(grads, part[rows_l:], preferred_element_type=jnp.float32),
        )

    h_mine, g_mine = project(mine, core)
    h_other, g_other = project(other, 1 - core)
    proj = jnp.concatenate([h_mine + h_other, g_mine + g_other], axis=1)

    share = tok_rows // X
    parts = lax.all_to_all(proj, "x", 0, 0, tiled=True).reshape(X, share, 4 * COLS)
    part = parts.sum(axis=0)
    h0, h1, g0, g1 = (part[:, i * COLS:(i + 1) * COLS] for i in range(4))
    first = hi == 0
    keep = jnp.concatenate([jnp.where(first, h0, h1), jnp.where(first, g0, g1)], axis=1)
    send = jnp.concatenate([jnp.where(first, h1, h0), jnp.where(first, g1, g0)], axis=1)
    full = keep + swap(send, "h")
    token_score = (full[:, :COLS] * full[:, COLS:]).reshape(share, QB, RANK).sum(axis=2)

    counts = doc_tokens[0]
    ends = jnp.cumsum(counts)
    starts = ends - counts
    places = jnp.arange(share, dtype=jnp.int32) + at_x * share
    inside = ((places[None, :] >= starts[:, None]) & (places[None, :] < ends[:, None])).astype(
        jnp.float32
    )
    partial = jnp.dot(
        inside, token_score, precision=lax.Precision.HIGHEST, preferred_element_type=jnp.float32
    )
    docs = partial.shape[0]
    flat = jnp.broadcast_to(partial.reshape(1, docs * QB), (H * X, docs * QB))
    every = lax.all_to_all(flat, ("h", "x"), 0, 0, tiled=True)
    summed = every.reshape(H, X, docs, QB).sum(axis=1)
    summed = jnp.concatenate([summed[0], summed[1]], axis=1)
    return summed / jnp.sqrt(jnp.float32(RANK * (tok_rows // 4)))


def solution(mesh):
    fine = Mesh(mesh.devices.reshape(Z, Y, C, H, X), ("z", "y", "c", "h", "x"))
    dp, tensor = ("z", "y", "c"), ("h", "x")
    return jax.shard_map(
        shards,
        mesh=fine,
        in_specs=(
            P(dp, tensor),
            P(dp, tensor),
            P(dp, tensor, None),
            P(dp, tensor, None),
            P(dp, None),
            P(),
        ),
        out_specs=P(dp, None),
        check_vma=False,
    )
```

```python
import jax
import jax.numpy as jnp
from jax import lax
from jax.sharding import Mesh
from jax.sharding import PartitionSpec as P

QB = 4
RANK = 32
COLS = QB * RANK
Z, Y, C, H, X = 8, 4, 2, 2, 4


def swap(block, axis):
    return lax.ppermute(block, axis, [(0, 1), (1, 0)])


def scatter(own):
    return lax.all_to_all(own, ("c", "z", "y"), 0, 0, tiled=True)


def pick(got, owners):
    picked = []
    for batch in range(2):
        owner = owners[batch]
        source = (owner % C) * (Z * Y) + owner // C
        picked.append(lax.dynamic_index_in_dim(got, source, 0, keepdims=False))
    return jnp.concatenate(picked, axis=1)


def gather(picked):
    piece, cols = picked.shape
    copies = jnp.broadcast_to(picked[None], (Z * Y, piece, cols)).reshape(Z * Y * piece, cols)
    return lax.all_to_all(copies, ("z", "y"), 0, 0, tiled=True)


def project(acts, mine, other, core):
    rows = mine.shape[0]
    near = lax.dynamic_slice_in_dim(acts, core * rows, rows, 1)
    far = lax.dynamic_slice_in_dim(acts, (1 - core) * rows, rows, 1)
    first = jnp.dot(near, mine, preferred_element_type=jnp.float32)
    first, other = lax.optimization_barrier((first, other))
    return first + jnp.dot(far, other, preferred_element_type=jnp.float32)


def reduce_tensor(proj):
    share = proj.shape[0] // X
    parts = lax.all_to_all(proj, "x", 0, 0, tiled=True).reshape(X, share, proj.shape[1])
    part = parts.sum(axis=0)
    return part + swap(part, "h")


def reduce_tensor_beside(proj, at_x):
    share = proj.shape[0] // X
    part = lax.dynamic_slice_in_dim(proj, at_x * share, share, 0)
    for step in range(1, X):
        rows = lax.dynamic_slice_in_dim(proj, lax.rem(at_x + step, X) * share, share, 0)
        part = part + lax.ppermute(rows, "x", [(i, (i + step) % X) for i in range(X)])
    return part + swap(part, "h")


def shards(hidden_acts, out_grads, left_factors, right_factors, doc_tokens, owners):
    tok_rows = hidden_acts.shape[0]
    core, at_x = lax.axis_index("c"), lax.axis_index("x")
    share = tok_rows // X

    members = Z * Y * C
    own_l = left_factors.reshape(members, -1, COLS)
    own_r = right_factors.reshape(members, -1, COLS)
    rows_r = own_r.shape[1]
    picked = pick(scatter(jnp.concatenate([own_r, own_l], axis=1)), owners)
    mine_r = gather(picked[:rows_r])
    picked_l, mine_r = lax.optimization_barrier((picked[rows_r:], mine_r))
    other_r = swap(mine_r, "c")
    full_g = reduce_tensor_beside(project(out_grads, mine_r, other_r, core), at_x)
    mine_l, full_g = lax.optimization_barrier((gather(picked_l), full_g))
    other_l = swap(mine_l, "c")

    full_h = reduce_tensor(project(hidden_acts, mine_l, other_l, core))
    token_score = (full_h * full_g).reshape(share, 2 * QB, RANK).sum(axis=2)

    counts = doc_tokens[0]
    ends = jnp.cumsum(counts)
    starts = ends - counts
    places = jnp.arange(share, dtype=jnp.int32) + at_x * share
    inside = ((places[None, :] >= starts[:, None]) & (places[None, :] < ends[:, None])).astype(
        jnp.float32
    )
    partial = jnp.dot(
        inside, token_score, precision=lax.Precision.HIGHEST, preferred_element_type=jnp.float32
    )
    docs, queries = partial.shape
    copies = jnp.broadcast_to(partial[None], (X, docs, queries)).reshape(X * docs, queries)
    summed = lax.all_to_all(copies, "x", 0, 0, tiled=True).reshape(X, docs, queries).sum(axis=0)
    return summed / jnp.sqrt(jnp.float32(RANK * (tok_rows // 4)))


def solution(mesh):
    fine = Mesh(mesh.devices.reshape(Z, Y, C, H, X), ("z", "y", "c", "h", "x"))
    dp, tensor = ("z", "y", "c"), ("h", "x")
    return jax.shard_map(
        shards,
        mesh=fine,
        in_specs=(
            P(dp, tensor),
            P(dp, tensor),
            P(dp, tensor, None),
            P(dp, tensor, None),
            P(dp, None),
            P(),
        ),
        out_specs=P(dp, None),
        check_vma=False,
    )
```

```python
import jax
import jax.numpy as jnp
from jax import lax
from jax.sharding import Mesh
from jax.sharding import PartitionSpec as P

QB = 4
RANK = 32
COLS = QB * RANK
Z, Y, C, H, X = 8, 4, 2, 2, 4


def swap(block, axis):
    return lax.ppermute(block, axis, [(0, 1), (1, 0)])


def turn(block, axis, size, step):
    return lax.ppermute(block, axis, [(i, (i + step) % size) for i in range(size)])


def scatter(own):
    members = Z * Y * C
    return lax.all_to_all(own.reshape(members, -1, COLS), ("c", "z", "y"), 0, 0, tiled=True)


def pick(got, owners):
    picked = []
    for batch in range(2):
        owner = owners[batch]
        source = (owner % C) * (Z * Y) + owner // C
        picked.append(lax.dynamic_index_in_dim(got, source, 0, keepdims=False))
    return jnp.concatenate(picked, axis=1)


def gather(picked):
    piece, cols = picked.shape
    copies = jnp.broadcast_to(picked[None], (Z * Y, piece, cols)).reshape(Z * Y * piece, cols)
    return lax.all_to_all(copies, ("z", "y"), 0, 0, tiled=True)


def project(acts, mine, other, core):
    rows = mine.shape[0]
    near = lax.dynamic_slice_in_dim(acts, core * rows, rows, 1)
    far = lax.dynamic_slice_in_dim(acts, (1 - core) * rows, rows, 1)
    first = jnp.dot(near, mine, preferred_element_type=jnp.float32)
    first, other = lax.optimization_barrier((first, other))
    return first + jnp.dot(far, other, preferred_element_type=jnp.float32)


def sum_x(proj, at_x):
    share = proj.shape[0] // X
    part = lax.dynamic_slice_in_dim(proj, at_x * share, share, 0)
    for step in range(1, X):
        rows = lax.dynamic_slice_in_dim(proj, lax.rem(at_x + step, X) * share, share, 0)
        part = part + turn(rows, "x", X, step)
    return part


def gather_x(part, at_x):
    share = part.shape[0]
    full = jnp.zeros((X * share, part.shape[1]), part.dtype)
    full = lax.dynamic_update_slice_in_dim(full, part, at_x * share, 0)
    for step in range(1, X):
        rows = turn(part, "x", X, step)
        full = lax.dynamic_update_slice_in_dim(full, rows, lax.rem(at_x - step + X, X) * share, 0)
    return full


def shards(hidden_acts, out_grads, left_factors, right_factors, doc_tokens, owners):
    tok_rows = hidden_acts.shape[0]
    core, at_x = lax.axis_index("c"), lax.axis_index("x")

    mine_r = gather(pick(scatter(right_factors), owners))
    left_factors, mine_r = lax.optimization_barrier((left_factors, mine_r))
    part_g = sum_x(project(out_grads, mine_r, swap(mine_r, "c"), core), at_x)
    got_l, part_g = lax.optimization_barrier((scatter(left_factors), part_g))
    full_g = gather_x(part_g + swap(part_g, "h"), at_x)
    mine_l, full_g = lax.optimization_barrier((gather(pick(got_l, owners)), full_g))

    part_h = project(hidden_acts, mine_l, swap(mine_l, "c"), core)
    token_score = (part_h * full_g).reshape(tok_rows, 2 * QB, RANK).sum(axis=2)

    counts = doc_tokens[0]
    ends = jnp.cumsum(counts)
    starts = ends - counts
    places = jnp.arange(tok_rows, dtype=jnp.int32)
    inside = ((places[None, :] >= starts[:, None]) & (places[None, :] < ends[:, None])).astype(
        jnp.float32
    )
    partial = jnp.dot(
        inside, token_score, precision=lax.Precision.HIGHEST, preferred_element_type=jnp.float32
    )
    docs, queries = partial.shape
    copies = jnp.broadcast_to(partial[None], (H * X, docs, queries))
    summed = lax.all_to_all(copies, ("h", "x"), 0, 0, tiled=True).sum(axis=0)
    return summed / jnp.sqrt(jnp.float32(RANK * (tok_rows // 4)))


def solution(mesh):
    fine = Mesh(mesh.devices.reshape(Z, Y, C, H, X), ("z", "y", "c", "h", "x"))
    dp, tensor = ("z", "y", "c"), ("h", "x")
    return jax.shard_map(
        shards,
        mesh=fine,
        in_specs=(
            P(dp, tensor),
            P(dp, tensor),
            P(dp, tensor, None),
            P(dp, tensor, None),
            P(dp, None),
            P(),
        ),
        out_specs=P(dp, None),
        check_vma=False,
    )
```

```python
import jax
import jax.numpy as jnp
from jax import lax
from jax.sharding import Mesh
from jax.sharding import PartitionSpec as P

QB = 4
RANK = 32
COLS = QB * RANK
Z, Y, C, H, X = 8, 4, 2, 2, 4


def swap(block, axis):
    return lax.ppermute(block, axis, [(0, 1), (1, 0)])


def turn(block, axis, size, step):
    return lax.ppermute(block, axis, [(i, (i + step) % size) for i in range(size)])


def scatter(own):
    members = Z * Y * C
    return lax.all_to_all(own.reshape(members, -1, COLS), ("c", "z", "y"), 0, 0, tiled=True)


def pick(got, owners):
    picked = []
    for batch in range(2):
        owner = owners[batch]
        source = (owner % C) * (Z * Y) + owner // C
        picked.append(lax.dynamic_index_in_dim(got, source, 0, keepdims=False))
    return jnp.concatenate(picked, axis=1)


def gather(picked):
    piece, cols = picked.shape
    copies = jnp.broadcast_to(picked[None], (Z * Y, piece, cols)).reshape(Z * Y * piece, cols)
    return lax.all_to_all(copies, ("z", "y"), 0, 0, tiled=True)


def project(acts, mine, other, core):
    rows = mine.shape[0]
    near = lax.dynamic_slice_in_dim(acts, core * rows, rows, 1)
    far = lax.dynamic_slice_in_dim(acts, (1 - core) * rows, rows, 1)
    first = jnp.dot(near, mine, preferred_element_type=jnp.float32)
    first, other = lax.optimization_barrier((first, other))
    return first + jnp.dot(far, other, preferred_element_type=jnp.float32)


def sum_x(proj, at_x):
    share = proj.shape[0] // X
    part = lax.dynamic_slice_in_dim(proj, at_x * share, share, 0)
    for step in range(1, X):
        rows = lax.dynamic_slice_in_dim(proj, lax.rem(at_x + step, X) * share, share, 0)
        part = part + turn(rows, "x", X, step)
    return part


def shards(hidden_acts, out_grads, left_factors, right_factors, doc_tokens, owners):
    tok_rows = hidden_acts.shape[0]
    core, at_x = lax.axis_index("c"), lax.axis_index("x")

    mine_r = gather(pick(scatter(right_factors), owners))
    left_factors, mine_r = lax.optimization_barrier((left_factors, mine_r))
    part_g = sum_x(project(out_grads, mine_r, swap(mine_r, "c"), core), at_x)
    other_g = swap(part_g, "h")
    got_l, part_g = lax.optimization_barrier((scatter(left_factors), part_g))
    full_g = lax.all_gather(part_g + other_g, "x", axis=0, tiled=True)
    mine_l, full_g = lax.optimization_barrier((gather(pick(got_l, owners)), full_g))

    part_h = project(hidden_acts, mine_l, swap(mine_l, "c"), core)
    token_score = (part_h * full_g).reshape(tok_rows, 2 * QB, RANK).sum(axis=2)

    counts = doc_tokens[0]
    ends = jnp.cumsum(counts)
    starts = ends - counts
    places = jnp.arange(tok_rows, dtype=jnp.int32)
    inside = ((places[None, :] >= starts[:, None]) & (places[None, :] < ends[:, None])).astype(
        jnp.float32
    )
    partial = jnp.dot(
        inside, token_score, precision=lax.Precision.HIGHEST, preferred_element_type=jnp.float32
    )
    docs, queries = partial.shape
    copies = jnp.broadcast_to(partial[None], (H * X, docs, queries))
    summed = lax.all_to_all(copies, ("h", "x"), 0, 0, tiled=True).sum(axis=0)
    return summed / jnp.sqrt(jnp.float32(RANK * (tok_rows // 4)))


def solution(mesh):
    fine = Mesh(mesh.devices.reshape(Z, Y, C, H, X), ("z", "y", "c", "h", "x"))
    dp, tensor = ("z", "y", "c"), ("h", "x")
    return jax.shard_map(
        shards,
        mesh=fine,
        in_specs=(
            P(dp, tensor),
            P(dp, tensor),
            P(dp, tensor, None),
            P(dp, tensor, None),
            P(dp, None),
            P(),
        ),
        out_specs=P(dp, None),
        check_vma=False,
    )
```

```python
import jax
import jax.numpy as jnp
from jax import lax
from jax.sharding import Mesh
from jax.sharding import PartitionSpec as P

QB = 4
RANK = 32
COLS = QB * RANK
Z, Y, C, H, X = 8, 4, 2, 2, 4


def swap(block, axis):
    return lax.ppermute(block, axis, [(0, 1), (1, 0)])


def turn(block, axis, size, step):
    return lax.ppermute(block, axis, [(i, (i + step) % size) for i in range(size)])


def scatter(own):
    members = Z * Y * C
    return lax.all_to_all(own.reshape(members, -1, COLS), ("c", "z", "y"), 0, 0, tiled=True)


def pick(got, owners):
    picked = []
    for batch in range(2):
        owner = owners[batch]
        source = (owner % C) * (Z * Y) + owner // C
        picked.append(lax.dynamic_index_in_dim(got, source, 0, keepdims=False))
    return jnp.concatenate(picked, axis=1)


def gather(picked):
    piece, cols = picked.shape
    copies = jnp.broadcast_to(picked[None], (Z * Y, piece, cols)).reshape(Z * Y * piece, cols)
    return lax.all_to_all(copies, ("z", "y"), 0, 0, tiled=True)


def project(acts, mine, other, core):
    rows = mine.shape[0]
    near = lax.dynamic_slice_in_dim(acts, core * rows, rows, 1)
    far = lax.dynamic_slice_in_dim(acts, (1 - core) * rows, rows, 1)
    first = jnp.dot(near, mine, preferred_element_type=jnp.float32)
    first, other = lax.optimization_barrier((first, other))
    return first + jnp.dot(far, other, preferred_element_type=jnp.float32)


def sum_x(proj, at_x):
    share = proj.shape[0] // X
    part = lax.dynamic_slice_in_dim(proj, at_x * share, share, 0)
    for step in range(1, X):
        rows = lax.dynamic_slice_in_dim(proj, lax.rem(at_x + step, X) * share, share, 0)
        part = part + turn(rows, "x", X, step)
    return part


def shards(hidden_acts, out_grads, left_factors, right_factors, doc_tokens, owners):
    tok_rows = hidden_acts.shape[0]
    core, at_x = lax.axis_index("c"), lax.axis_index("x")

    mine_r = gather(pick(scatter(right_factors), owners))
    left_factors, mine_r = lax.optimization_barrier((left_factors, mine_r))
    part_g = sum_x(project(out_grads, mine_r, swap(mine_r, "c"), core), at_x)
    picked_l = pick(scatter(left_factors), owners)
    picked_l, part_g = lax.optimization_barrier((picked_l, part_g + swap(part_g, "h")))
    full_g = lax.all_gather(part_g, "x", axis=0, tiled=True)
    mine_l, full_g = lax.optimization_barrier((gather(picked_l), full_g))

    part_h = project(hidden_acts, mine_l, swap(mine_l, "c"), core)
    token_score = (part_h * full_g).reshape(tok_rows, 2 * QB, RANK).sum(axis=2)

    counts = doc_tokens[0]
    ends = jnp.cumsum(counts)
    starts = ends - counts
    places = jnp.arange(tok_rows, dtype=jnp.int32)
    inside = ((places[None, :] >= starts[:, None]) & (places[None, :] < ends[:, None])).astype(
        jnp.float32
    )
    partial = jnp.dot(
        inside, token_score, precision=lax.Precision.HIGHEST, preferred_element_type=jnp.float32
    )
    docs, queries = partial.shape
    copies = jnp.broadcast_to(partial[None], (H * X, docs, queries))
    summed = lax.all_to_all(copies, ("h", "x"), 0, 0, tiled=True).sum(axis=0)
    return summed / jnp.sqrt(jnp.float32(RANK * (tok_rows // 4)))


def solution(mesh):
    fine = Mesh(mesh.devices.reshape(Z, Y, C, H, X), ("z", "y", "c", "h", "x"))
    dp, tensor = ("z", "y", "c"), ("h", "x")
    return jax.shard_map(
        shards,
        mesh=fine,
        in_specs=(
            P(dp, tensor),
            P(dp, tensor),
            P(dp, tensor, None),
            P(dp, tensor, None),
            P(dp, None),
            P(),
        ),
        out_specs=P(dp, None),
        check_vma=False,
    )
```

```python
import jax
import jax.numpy as jnp
from jax import lax
from jax.sharding import Mesh
from jax.sharding import PartitionSpec as P

QB = 4
RANK = 32
COLS = QB * RANK
Z, Y, C, H, X = 8, 4, 2, 2, 4


def swap(block, axis):
    return lax.ppermute(block, axis, [(0, 1), (1, 0)])


def pick(got, owners):
    picked = []
    for batch in range(2):
        owner = owners[batch]
        source = (owner % C) * (Z * Y) + owner // C
        picked.append(lax.dynamic_index_in_dim(got, source, 0, keepdims=False))
    return jnp.concatenate(picked, axis=1)


def dot(acts, part, side):
    rows = part.shape[0]
    acts = lax.dynamic_slice_in_dim(acts, side * rows, rows, 1)
    return jnp.dot(acts, part, preferred_element_type=jnp.float32)


def sum_x(proj):
    parts = lax.all_to_all(proj, "x", 0, 0, tiled=True)
    return parts.reshape(X, -1, proj.shape[1]).sum(axis=0)


def shards(hidden_acts, out_grads, left_factors, right_factors, doc_tokens, owners):
    tok_rows = hidden_acts.shape[0]
    core, at_x = lax.axis_index("c"), lax.axis_index("x")
    share = tok_rows // X

    right, left = right_factors[0], left_factors[0]
    rows_r, rows_l = right.shape[0] // C, left.shape[0] // C
    own = jnp.concatenate([right[:rows_r], left[:rows_l], right[rows_r:], left[rows_l:]], axis=0)
    own = own.reshape(Z * Y * C, -1, COLS)
    picked = pick(lax.all_to_all(own, ("c", "z", "y"), 0, 0, tiled=True), owners)

    copies = jnp.broadcast_to(picked[None], (Z * Y, *picked.shape))
    mine = lax.all_to_all(copies, ("z", "y"), 0, 0, tiled=True).reshape(-1, 2 * COLS)
    other = swap(mine, "c")

    near_g = dot(out_grads, mine[:rows_r], core)
    near_h = dot(hidden_acts, mine[rows_r:], core)
    near_g, near_h, other = lax.optimization_barrier((near_g, near_h, other))
    proj_g = near_g + dot(out_grads, other[:rows_r], 1 - core)
    proj_h = near_h + dot(hidden_acts, other[rows_r:], 1 - core)

    part_g = sum_x(proj_g)
    part_h = sum_x(proj_h)
    full_g = part_g + swap(part_g, "h")
    full_h = part_h + swap(part_h, "h")
    token_score = (full_h * full_g).reshape(share, 2 * QB, RANK).sum(axis=2)

    counts = doc_tokens[0]
    ends = jnp.cumsum(counts)
    starts = ends - counts
    places = jnp.arange(share, dtype=jnp.int32) + at_x * share
    inside = ((places[None, :] >= starts[:, None]) & (places[None, :] < ends[:, None])).astype(
        jnp.float32
    )
    partial = jnp.dot(
        inside, token_score, precision=lax.Precision.HIGHEST, preferred_element_type=jnp.float32
    )
    copies = jnp.broadcast_to(partial[None], (X, *partial.shape))
    summed = lax.all_to_all(copies, "x", 0, 0, tiled=True).sum(axis=0)
    return summed / jnp.sqrt(jnp.float32(RANK * (tok_rows // 4)))


def solution(mesh):
    fine = Mesh(mesh.devices.reshape(Z, Y, C, H, X), ("z", "y", "c", "h", "x"))
    dp, tensor = ("z", "y", "c"), ("h", "x")
    return jax.shard_map(
        shards,
        mesh=fine,
        in_specs=(
            P(dp, tensor),
            P(dp, tensor),
            P(dp, tensor, None),
            P(dp, tensor, None),
            P(dp, None),
            P(),
        ),
        out_specs=P(dp, None),
        check_vma=False,
    )
```

```python
import jax
import jax.numpy as jnp
from jax import lax
from jax.sharding import Mesh
from jax.sharding import PartitionSpec as P

QB = 4
RANK = 32
COLS = QB * RANK
Z, Y, C, H, X = 8, 4, 2, 2, 4


def swap(block, axis):
    return lax.ppermute(block, axis, [(0, 1), (1, 0)])


def pick(got, sources):
    picked = [lax.dynamic_index_in_dim(got, source, 0, keepdims=False) for source in sources]
    return jnp.concatenate(picked, axis=1)


def scatter_cores(right, left, owners):
    rows_r, rows_l = right.shape[0] // C, left.shape[0] // C
    own = jnp.concatenate([right[:rows_r], left[:rows_l], right[rows_r:], left[rows_l:]], axis=0)
    own = own.reshape(Z * Y * C, -1, COLS)
    got = lax.all_to_all(own, ("c", "z", "y"), 0, 0, tiled=True)
    return pick(got, [(owner % C) * (Z * Y) + owner // C for owner in owners])


def scatter_chips(right, left, owners):
    core, chip = lax.axis_index("c"), lax.axis_index(("z", "y"))
    rows_r, rows_l = right.shape[0] // C, left.shape[0] // C

    def half(side):
        return (
            lax.dynamic_slice_in_dim(right, side * rows_r, rows_r, 0),
            lax.dynamic_slice_in_dim(left, side * rows_l, rows_l, 0),
        )

    far = swap(jnp.concatenate(half(1 - core), axis=0), "c")
    wanted = jnp.where(chip == owners[0] // C, owners[0] % C, owners[1] % C)
    mine = jnp.where(wanted == core, jnp.concatenate(half(core), axis=0), far)
    got = lax.all_to_all(mine.reshape(Z * Y, -1, COLS), ("z", "y"), 0, 0, tiled=True)
    return pick(got, [owner // C for owner in owners])


def dot(acts, part, side):
    rows = part.shape[0]
    acts = lax.dynamic_slice_in_dim(acts, side * rows, rows, 1)
    return jnp.dot(acts, part, preferred_element_type=jnp.float32)


def sum_x(proj):
    parts = lax.all_to_all(proj, "x", 0, 0, tiled=True)
    return parts.reshape(X, -1, proj.shape[1]).sum(axis=0)


def shards(hidden_acts, out_grads, left_factors, right_factors, doc_tokens, owners):
    tok_rows = hidden_acts.shape[0]
    core, at_x = lax.axis_index("c"), lax.axis_index("x")
    share = tok_rows // X

    right, left = right_factors[0], left_factors[0]
    rows_r = right.shape[0] // C
    owner = owners[0], owners[1]
    two_cores = (owner[0] // C == owner[1] // C) & (owner[0] != owner[1])
    picked = lax.cond(two_cores, scatter_cores, scatter_chips, right, left, owner)

    copies = jnp.broadcast_to(picked[None], (Z * Y, *picked.shape))
    mine = lax.all_to_all(copies, ("z", "y"), 0, 0, tiled=True).reshape(-1, 2 * COLS)
    other = swap(mine, "c")

    near_g = dot(out_grads, mine[:rows_r], core)
    near_h = dot(hidden_acts, mine[rows_r:], core)
    near_g, near_h, other = lax.optimization_barrier((near_g, near_h, other))
    proj_g = near_g + dot(out_grads, other[:rows_r], 1 - core)
    proj_h = near_h + dot(hidden_acts, other[rows_r:], 1 - core)

    part = sum_x(jnp.concatenate([proj_g, proj_h], axis=1))
    full = part + swap(part, "h")
    full_g, full_h = full[:, : 2 * COLS], full[:, 2 * COLS :]
    token_score = (full_h * full_g).reshape(share, 2 * QB, RANK).sum(axis=2)

    counts = doc_tokens[0]
    ends = jnp.cumsum(counts)
    starts = ends - counts
    places = jnp.arange(share, dtype=jnp.int32) + at_x * share
    inside = ((places[None, :] >= starts[:, None]) & (places[None, :] < ends[:, None])).astype(
        jnp.float32
    )
    partial = jnp.dot(
        inside, token_score, precision=lax.Precision.HIGHEST, preferred_element_type=jnp.float32
    )
    copies = jnp.broadcast_to(partial[None], (X, *partial.shape))
    summed = lax.all_to_all(copies, "x", 0, 0, tiled=True).sum(axis=0)
    return summed / jnp.sqrt(jnp.float32(RANK * (tok_rows // 4)))


def solution(mesh):
    fine = Mesh(mesh.devices.reshape(Z, Y, C, H, X), ("z", "y", "c", "h", "x"))
    dp, tensor = ("z", "y", "c"), ("h", "x")
    return jax.shard_map(
        shards,
        mesh=fine,
        in_specs=(
            P(dp, tensor),
            P(dp, tensor),
            P(dp, tensor, None),
            P(dp, tensor, None),
            P(dp, None),
            P(),
        ),
        out_specs=P(dp, None),
        check_vma=False,
    )
```

```python
import jax
import jax.numpy as jnp
from jax import lax
from jax.sharding import Mesh
from jax.sharding import PartitionSpec as P

QB = 4
RANK = 32
COLS = QB * RANK
Z, Y, C, H, X = 8, 4, 2, 2, 4


def swap(block, axis):
    return lax.ppermute(block, axis, [(0, 1), (1, 0)])


def cut(block, start, size, axis):
    return lax.dynamic_slice_in_dim(block, start, size, axis, allow_negative_indices=False)


def pick(got, sources):
    return jnp.concatenate([cut(got, source, 1, 0)[0] for source in sources], axis=1)


def scatter_cores(right, left, owners):
    rows_r, rows_l = right.shape[0] // C, left.shape[0] // C
    own = jnp.concatenate([right[:rows_r], left[:rows_l], right[rows_r:], left[rows_l:]], axis=0)
    own = own.reshape(Z * Y * C, -1, COLS)
    got = lax.all_to_all(own, ("c", "z", "y"), 0, 0, tiled=True)
    return pick(got, [(owner & 1) * (Z * Y) + (owner >> 1) for owner in owners])


def scatter_chips(right, left, owners):
    core, chip = lax.axis_index("c"), lax.axis_index(("z", "y"))
    rows_r, rows_l = right.shape[0] // C, left.shape[0] // C

    def half(side):
        return (
            cut(right, side * rows_r, rows_r, 0),
            cut(left, side * rows_l, rows_l, 0),
        )

    far = swap(jnp.concatenate(half(1 - core), axis=0), "c")
    wanted = jnp.where(chip == owners[0] >> 1, owners[0], owners[1]) & 1
    mine = jnp.where(wanted == core, jnp.concatenate(half(core), axis=0), far)
    got = lax.all_to_all(mine.reshape(Z * Y, -1, COLS), ("z", "y"), 0, 0, tiled=True)
    return pick(got, [owner >> 1 for owner in owners])


def dot(acts, part, side):
    rows = part.shape[0]
    acts = cut(acts, side * rows, rows, 1)
    return jnp.dot(acts, part, preferred_element_type=jnp.float32)


def sum_x(proj):
    parts = lax.all_to_all(proj, "x", 0, 0, tiled=True)
    return parts.reshape(X, -1, proj.shape[1]).sum(axis=0)


def shards(hidden_acts, out_grads, left_factors, right_factors, doc_tokens, owners):
    tok_rows = hidden_acts.shape[0]
    core, at_x = lax.axis_index("c"), lax.axis_index("x")
    share = tok_rows // X

    right, left = right_factors[0], left_factors[0]
    rows_r = right.shape[0] // C
    owner = owners[0], owners[1]
    picked = lax.cond(owner[0] ^ owner[1] == 1, scatter_cores, scatter_chips, right, left, owner)

    copies = jnp.broadcast_to(picked[None], (Z * Y, *picked.shape))
    mine = lax.all_to_all(copies, ("z", "y"), 0, 0, tiled=True).reshape(-1, 2 * COLS)
    other = swap(mine, "c")

    near_g = dot(out_grads, mine[:rows_r], core)
    near_h = dot(hidden_acts, mine[rows_r:], core)
    near_g, near_h, other = lax.optimization_barrier((near_g, near_h, other))
    proj_g = near_g + dot(out_grads, other[:rows_r], 1 - core)
    proj_h = near_h + dot(hidden_acts, other[rows_r:], 1 - core)

    part_g = sum_x(proj_g)
    part_h = sum_x(proj_h)
    full_g = part_g + swap(part_g, "h")
    full_h = part_h + swap(part_h, "h")
    token_score = (full_h * full_g).reshape(share, 2 * QB, RANK).sum(axis=2)

    counts = doc_tokens[0]
    ends = jnp.cumsum(counts)
    starts = ends - counts
    places = jnp.arange(share, dtype=jnp.int32) + at_x * share
    inside = ((places[None, :] >= starts[:, None]) & (places[None, :] < ends[:, None])).astype(
        jnp.float32
    )
    partial = jnp.dot(
        inside, token_score, precision=lax.Precision.HIGHEST, preferred_element_type=jnp.float32
    )
    copies = jnp.broadcast_to(partial[None], (X, *partial.shape))
    summed = lax.all_to_all(copies, "x", 0, 0, tiled=True).sum(axis=0)
    return summed / jnp.sqrt(jnp.float32(RANK * (tok_rows // 4)))


def solution(mesh):
    fine = Mesh(mesh.devices.reshape(Z, Y, C, H, X), ("z", "y", "c", "h", "x"))
    dp, tensor = ("z", "y", "c"), ("h", "x")
    return jax.shard_map(
        shards,
        mesh=fine,
        in_specs=(
            P(dp, tensor),
            P(dp, tensor),
            P(dp, tensor, None),
            P(dp, tensor, None),
            P(dp, None),
            P(),
        ),
        out_specs=P(dp, None),
        check_vma=False,
    )
```

```python
import jax
import jax.numpy as jnp
from jax import lax
from jax.sharding import Mesh
from jax.sharding import PartitionSpec as P

QB = 4
RANK = 32
COLS = QB * RANK
Z, Y, C, H, X = 8, 4, 2, 2, 4


def swap(block, axis):
    return lax.ppermute(block, axis, [(0, 1), (1, 0)])


def cut(block, start, size, axis):
    return lax.dynamic_slice_in_dim(block, start, size, axis, allow_negative_indices=False)


def pick(got, sources):
    return jnp.concatenate([cut(got, source, 1, 0)[0] for source in sources], axis=1)


def half(right, left, side):
    rows_r, rows_l = right.shape[0] // C, left.shape[0] // C
    return jnp.concatenate(
        [cut(right, side * rows_r, rows_r, 0), cut(left, side * rows_l, rows_l, 0)], axis=0
    )


def scatter_cores(right, left, mine, owners):
    own = jnp.concatenate([half(right, left, side) for side in range(C)], axis=0)
    own = own.reshape(Z * Y * C, -1, COLS)
    got = lax.all_to_all(own, ("c", "z", "y"), 0, 0, tiled=True)
    return pick(got, [(owner & 1) * (Z * Y) + (owner >> 1) for owner in owners])


def scatter_chips(right, left, mine, owners):
    got = lax.all_to_all(mine.reshape(Z * Y, -1, COLS), ("z", "y"), 0, 0, tiled=True)
    return pick(got, [owner >> 1 for owner in owners])


def dot(acts, part, side):
    rows = part.shape[0]
    acts = cut(acts, side * rows, rows, 1)
    return jnp.dot(acts, part, preferred_element_type=jnp.float32)


def sum_x(proj):
    parts = lax.all_to_all(proj, "x", 0, 0, tiled=True)
    return parts.reshape(X, -1, proj.shape[1]).sum(axis=0)


def shards(hidden_acts, out_grads, left_factors, right_factors, doc_tokens, owners):
    tok_rows = hidden_acts.shape[0]
    core, at_x = lax.axis_index("c"), lax.axis_index("x")
    chip = lax.axis_index(("z", "y"))
    share = tok_rows // X

    right, left = right_factors[0], left_factors[0]
    rows_r = right.shape[0] // C
    owner = owners[0], owners[1]
    far = swap(half(right, left, 1 - core), "c")
    wanted = jnp.where(chip == owner[0] >> 1, owner[0], owner[1]) & 1
    mine = jnp.where(wanted == core, half(right, left, core), far)
    picked = lax.cond(
        owner[0] ^ owner[1] == 1, scatter_cores, scatter_chips, right, left, mine, owner
    )

    copies = jnp.broadcast_to(picked[None], (Z * Y, *picked.shape))
    mine = lax.all_to_all(copies, ("z", "y"), 0, 0, tiled=True).reshape(-1, 2 * COLS)
    other = swap(mine, "c")

    near_g = dot(out_grads, mine[:rows_r], core)
    near_h = dot(hidden_acts, mine[rows_r:], core)
    proj_g = near_g + dot(out_grads, other[:rows_r], 1 - core)
    proj_h = near_h + dot(hidden_acts, other[rows_r:], 1 - core)

    part_g = sum_x(proj_g)
    part_h = sum_x(proj_h)
    full_g = part_g + swap(part_g, "h")
    full_h = part_h + swap(part_h, "h")
    token_score = (full_h * full_g).reshape(share, 2 * QB, RANK).sum(axis=2)

    counts = doc_tokens[0]
    ends = jnp.cumsum(counts)
    starts = ends - counts
    places = jnp.arange(share, dtype=jnp.int32) + at_x * share
    inside = ((places[None, :] >= starts[:, None]) & (places[None, :] < ends[:, None])).astype(
        jnp.float32
    )
    partial = jnp.dot(
        inside, token_score, precision=lax.Precision.HIGHEST, preferred_element_type=jnp.float32
    )
    copies = jnp.broadcast_to(partial[None], (X, *partial.shape))
    summed = lax.all_to_all(copies, "x", 0, 0, tiled=True).sum(axis=0)
    return summed / jnp.sqrt(jnp.float32(RANK * (tok_rows // 4)))


def solution(mesh):
    fine = Mesh(mesh.devices.reshape(Z, Y, C, H, X), ("z", "y", "c", "h", "x"))
    dp, tensor = ("z", "y", "c"), ("h", "x")
    return jax.shard_map(
        shards,
        mesh=fine,
        in_specs=(
            P(dp, tensor),
            P(dp, tensor),
            P(dp, tensor, None),
            P(dp, tensor, None),
            P(dp, None),
            P(),
        ),
        out_specs=P(dp, None),
        check_vma=False,
    )
```

```python
import jax
import jax.numpy as jnp
from jax import lax
from jax.experimental import pallas as pl
from jax.experimental.pallas import tpu as pltpu
from jax.sharding import Mesh
from jax.sharding import PartitionSpec as P

QB = 4
RANK = 32
COLS = QB * RANK
Z, Y, C, H, X = 8, 4, 2, 2, 4


def swap(block, axis):
    return lax.ppermute(block, axis, [(0, 1), (1, 0)])


def cut(block, start, size, axis):
    return lax.dynamic_slice_in_dim(block, start, size, axis, allow_negative_indices=False)


def pick(got, sources):
    return jnp.concatenate([cut(got, source, 1, 0)[0] for source in sources], axis=1)


def half(right, left, side):
    rows_r, rows_l = right.shape[0] // C, left.shape[0] // C
    return jnp.concatenate(
        [cut(right, side * rows_r, rows_r, 0), cut(left, side * rows_l, rows_l, 0)], axis=0
    )


LEFT_CUTS = 4


def half_copies(right, left, side, out, sems):
    rows_r, rows_l = right.shape[0] // C, left.shape[0] // C
    step = rows_l // LEFT_CUTS
    copies = []
    for i in range(LEFT_CUTS):
        start = pl.multiple_of(side * rows_l + i * step, step)
        copies.append(
            pltpu.make_async_copy(
                left.at[pl.ds(start, step)], out.at[pl.ds(rows_r + i * step, step)], sems.at[i]
            )
        )
    start = pl.multiple_of(side * rows_r, rows_r)
    copies.append(
        pltpu.make_async_copy(
            right.at[pl.ds(start, rows_r)], out.at[pl.ds(0, rows_r)], sems.at[LEFT_CUTS]
        )
    )
    return copies


def run(copies):
    for copy in copies:
        copy.start()
    for copy in copies:
        copy.wait()


def send_kernel(right, left, out, sems):
    run(half_copies(right, left, 1 - lax.axis_index("c"), out, sems))


def keep_kernel(owners, right, left, far, out, sems):
    core, chip = lax.axis_index("c"), lax.axis_index("z") * Y + lax.axis_index("y")
    wanted = jnp.where(chip == owners[0] >> 1, owners[0], owners[1]) & 1

    @pl.when(wanted == core)
    def _():
        run(half_copies(right, left, core, out, sems))

    @pl.when(wanted != core)
    def _():
        count = LEFT_CUTS
        step = out.shape[0] // count
        run(
            [
                pltpu.make_async_copy(
                    far.at[pl.ds(i * step, step)], out.at[pl.ds(i * step, step)], sems.at[i]
                )
                for i in range(count)
            ]
        )


def local_copy(kernel, right, left, *more, owners=None):
    rows = (right.shape[0] + left.shape[0]) // C
    operands = (right, left, *more)
    anywhere = pl.BlockSpec(memory_space=pl.ANY)
    in_specs = [anywhere] * len(operands)
    if owners is not None:
        operands = (owners, *operands)
        in_specs = [pl.BlockSpec(memory_space=pltpu.SMEM), *in_specs]
    return pl.pallas_call(
        kernel,
        out_shape=jax.ShapeDtypeStruct((rows, right.shape[1]), right.dtype),
        in_specs=in_specs,
        out_specs=anywhere,
        scratch_shapes=[pltpu.SemaphoreType.DMA((LEFT_CUTS + 1,))],
        cost_estimate=pl.CostEstimate(
            flops=0, bytes_accessed=4 * rows * right.shape[1], transcendentals=0
        ),
    )(*operands)


def scatter_cores(right, left, mine, owners):
    own = jnp.concatenate([half(right, left, side) for side in range(C)], axis=0)
    own = own.reshape(Z * Y * C, -1, COLS)
    got = lax.all_to_all(own, ("c", "z", "y"), 0, 0, tiled=True)
    return pick(got, [(owner & 1) * (Z * Y) + (owner >> 1) for owner in owners])


def scatter_chips(right, left, mine, owners):
    got = lax.all_to_all(mine.reshape(Z * Y, -1, COLS), ("z", "y"), 0, 0, tiled=True)
    return pick(got, [owner >> 1 for owner in owners])


def dot(acts, part, side):
    rows = part.shape[0]
    acts = cut(acts, side * rows, rows, 1)
    return jnp.dot(acts, part, preferred_element_type=jnp.float32)


def sum_x(proj):
    parts = lax.all_to_all(proj, "x", 0, 0, tiled=True)
    return parts.reshape(X, -1, proj.shape[1]).sum(axis=0)


def shards(hidden_acts, out_grads, left_factors, right_factors, doc_tokens, owners):
    tok_rows = hidden_acts.shape[0]
    core, at_x = lax.axis_index("c"), lax.axis_index("x")
    share = tok_rows // X

    right, left = right_factors[0], left_factors[0]
    rows_r = right.shape[0] // C
    owner = owners[0], owners[1]
    far = swap(local_copy(send_kernel, right, left), "c")
    mine = local_copy(keep_kernel, right, left, far, owners=owners)
    picked = lax.cond(
        owner[0] ^ owner[1] == 1, scatter_cores, scatter_chips, right, left, mine, owner
    )

    copies = jnp.broadcast_to(picked[None], (Z * Y, *picked.shape))
    mine = lax.all_to_all(copies, ("z", "y"), 0, 0, tiled=True).reshape(-1, 2 * COLS)
    other = swap(mine, "c")

    near_g = dot(out_grads, mine[:rows_r], core)
    near_h = dot(hidden_acts, mine[rows_r:], core)
    proj_g = near_g + dot(out_grads, other[:rows_r], 1 - core)
    proj_h = near_h + dot(hidden_acts, other[rows_r:], 1 - core)

    part_g = sum_x(proj_g)
    part_h = sum_x(proj_h)
    full_g = part_g + swap(part_g, "h")
    full_h = part_h + swap(part_h, "h")
    token_score = (full_h * full_g).reshape(share, 2 * QB, RANK).sum(axis=2)

    counts = doc_tokens[0]
    ends = jnp.cumsum(counts)
    starts = ends - counts
    places = jnp.arange(share, dtype=jnp.int32) + at_x * share
    inside = ((places[None, :] >= starts[:, None]) & (places[None, :] < ends[:, None])).astype(
        jnp.float32
    )
    partial = jnp.dot(
        inside, token_score, precision=lax.Precision.HIGHEST, preferred_element_type=jnp.float32
    )
    copies = jnp.broadcast_to(partial[None], (X, *partial.shape))
    summed = lax.all_to_all(copies, "x", 0, 0, tiled=True).sum(axis=0)
    return summed / jnp.sqrt(jnp.float32(RANK * (tok_rows // 4)))


def solution(mesh):
    fine = Mesh(mesh.devices.reshape(Z, Y, C, H, X), ("z", "y", "c", "h", "x"))
    dp, tensor = ("z", "y", "c"), ("h", "x")
    return jax.shard_map(
        shards,
        mesh=fine,
        in_specs=(
            P(dp, tensor),
            P(dp, tensor),
            P(dp, tensor, None),
            P(dp, tensor, None),
            P(dp, None),
            P(),
        ),
        out_specs=P(dp, None),
        check_vma=False,
    )
```

```python
import jax
import jax.numpy as jnp
from jax import lax
from jax.sharding import Mesh
from jax.sharding import PartitionSpec as P

QB = 4
RANK = 32
COLS = QB * RANK
Z, Y, C, H, X = 8, 4, 2, 2, 4


def swap(block, axis):
    return lax.ppermute(block, axis, [(0, 1), (1, 0)])


def cut(block, start, size, axis):
    return lax.dynamic_slice_in_dim(block, start, size, axis, allow_negative_indices=False)


def pick(got, sources):
    return jnp.concatenate([cut(got, source, 1, 0)[0] for source in sources], axis=1)


def halves(factor, core):
    rows = factor.shape[0] // C
    low, high = factor[:rows], factor[rows:]
    return jnp.where(core == 0, low, high), jnp.where(core == 0, high, low)


def scatter_cores(right, left, mine, owners):
    rows_r, rows_l = right.shape[0] // C, left.shape[0] // C
    own = jnp.concatenate([right[:rows_r], left[:rows_l], right[rows_r:], left[rows_l:]], axis=0)
    own = own.reshape(Z * Y * C, -1, COLS)
    got = lax.all_to_all(own, ("c", "z", "y"), 0, 0, tiled=True)
    return pick(got, [(owner & 1) * (Z * Y) + (owner >> 1) for owner in owners])


def scatter_chips(right, left, mine, owners):
    got = lax.all_to_all(mine.reshape(Z * Y, -1, COLS), ("z", "y"), 0, 0, tiled=True)
    return pick(got, [owner >> 1 for owner in owners])


def dot(acts, part, side):
    rows = part.shape[0]
    acts = cut(acts, side * rows, rows, 1)
    return jnp.dot(acts, part, preferred_element_type=jnp.float32)


def sum_x(proj):
    parts = lax.all_to_all(proj, "x", 0, 0, tiled=True)
    return parts.reshape(X, -1, proj.shape[1]).sum(axis=0)


def shards(hidden_acts, out_grads, left_factors, right_factors, doc_tokens, owners):
    tok_rows = hidden_acts.shape[0]
    core, at_x = lax.axis_index("c"), lax.axis_index("x")
    chip = lax.axis_index(("z", "y"))
    share = tok_rows // X

    right, left = right_factors[0], left_factors[0]
    rows_r = right.shape[0] // C
    owner = owners[0], owners[1]
    near_r, send_r = halves(right, core)
    near_l, send_l = halves(left, core)
    far = swap(jnp.concatenate([send_r, send_l], axis=0), "c")
    wanted = (jnp.where(chip == owner[0] >> 1, owner[0], owner[1]) & 1) == core
    mine = jnp.concatenate(
        [jnp.where(wanted, near_r, far[:rows_r]), jnp.where(wanted, near_l, far[rows_r:])], axis=0
    )
    picked = lax.cond(
        owner[0] ^ owner[1] == 1, scatter_cores, scatter_chips, right, left, mine, owner
    )

    copies = jnp.broadcast_to(picked[None], (Z * Y, *picked.shape))
    mine = lax.all_to_all(copies, ("z", "y"), 0, 0, tiled=True).reshape(-1, 2 * COLS)
    other = swap(mine, "c")

    near_g = dot(out_grads, mine[:rows_r], core)
    near_h = dot(hidden_acts, mine[rows_r:], core)
    proj_g = near_g + dot(out_grads, other[:rows_r], 1 - core)
    proj_h = near_h + dot(hidden_acts, other[rows_r:], 1 - core)

    part_g = sum_x(proj_g)
    part_h = sum_x(proj_h)
    full_g = part_g + swap(part_g, "h")
    full_h = part_h + swap(part_h, "h")
    token_score = (full_h * full_g).reshape(share, 2 * QB, RANK).sum(axis=2)

    counts = doc_tokens[0]
    ends = jnp.cumsum(counts)
    starts = ends - counts
    places = jnp.arange(share, dtype=jnp.int32) + at_x * share
    inside = ((places[None, :] >= starts[:, None]) & (places[None, :] < ends[:, None])).astype(
        jnp.float32
    )
    partial = jnp.dot(
        inside, token_score, precision=lax.Precision.HIGHEST, preferred_element_type=jnp.float32
    )
    copies = jnp.broadcast_to(partial[None], (X, *partial.shape))
    summed = lax.all_to_all(copies, "x", 0, 0, tiled=True).sum(axis=0)
    return summed / jnp.sqrt(jnp.float32(RANK * (tok_rows // 4)))


def solution(mesh):
    fine = Mesh(mesh.devices.reshape(Z, Y, C, H, X), ("z", "y", "c", "h", "x"))
    dp, tensor = ("z", "y", "c"), ("h", "x")
    return jax.shard_map(
        shards,
        mesh=fine,
        in_specs=(
            P(dp, tensor),
            P(dp, tensor),
            P(dp, tensor, None),
            P(dp, tensor, None),
            P(dp, None),
            P(),
        ),
        out_specs=P(dp, None),
        check_vma=False,
    )
```

```python
import jax
import jax.numpy as jnp
from jax import lax
from jax.sharding import Mesh
from jax.sharding import PartitionSpec as P

QB = 4
RANK = 32
COLS = QB * RANK
Z, Y, C, H, X = 8, 4, 2, 2, 4


def swap(block, axis):
    return lax.ppermute(block, axis, [(0, 1), (1, 0)])


def cut(block, start, size, axis):
    return lax.dynamic_slice_in_dim(block, start, size, axis, allow_negative_indices=False)


def pick(got, sources):
    return jnp.concatenate([cut(got, source, 1, 0)[0] for source in sources], axis=1)


def half(right, left, side):
    rows_r, rows_l = right.shape[0] // C, left.shape[0] // C
    return jnp.concatenate(
        [cut(right, side * rows_r, rows_r, 0), cut(left, side * rows_l, rows_l, 0)], axis=0
    )


def scatter_cores(right, left, mine, owners):
    own = jnp.concatenate([half(right, left, side) for side in range(C)], axis=0)
    own = own.reshape(Z * Y * C, -1, COLS)
    got = lax.all_to_all(own, ("c", "z", "y"), 0, 0, tiled=True)
    return pick(got, [(owner & 1) * (Z * Y) + (owner >> 1) for owner in owners])


def scatter_chips(right, left, mine, owners):
    got = lax.all_to_all(mine.reshape(Z * Y, -1, COLS), ("z", "y"), 0, 0, tiled=True)
    return pick(got, [owner >> 1 for owner in owners])


def dot(acts, part, side):
    rows = part.shape[0]
    acts = cut(acts, side * rows, rows, 1)
    return jnp.dot(acts, part, preferred_element_type=jnp.float32)


def sum_x(proj):
    parts = lax.all_to_all(proj, "x", 0, 0, tiled=True)
    return parts.reshape(X, -1, proj.shape[1]).sum(axis=0)


def shards(hidden_acts, out_grads, left_factors, right_factors, doc_tokens, owners):
    tok_rows = hidden_acts.shape[0]
    core, at_x = lax.axis_index("c"), lax.axis_index("x")
    device = lax.axis_index(("z", "y", "c"))
    share = tok_rows // X

    right, left = right_factors[0], left_factors[0]
    rows_r = right.shape[0] // C
    owner = owners[0], owners[1]
    far = swap(half(right, left, 1 - core), "c")
    wanted = (owner[0] == device) | (owner[1] == device)
    rows_l = left.shape[0] // C
    near_r, near_l = cut(right, core * rows_r, rows_r, 0), cut(left, core * rows_l, rows_l, 0)
    mine = jnp.concatenate(
        [jnp.where(wanted, near_r, far[:rows_r]), jnp.where(wanted, near_l, far[rows_r:])], axis=0
    )
    picked = lax.cond(
        owner[0] ^ owner[1] == 1, scatter_cores, scatter_chips, right, left, mine, owner
    )

    copies = jnp.broadcast_to(picked[None], (Z * Y, *picked.shape))
    mine = lax.all_to_all(copies, ("z", "y"), 0, 0, tiled=True).reshape(-1, 2 * COLS)
    other = swap(mine, "c")

    near_g = dot(out_grads, mine[:rows_r], core)
    near_h = dot(hidden_acts, mine[rows_r:], core)
    proj_g = near_g + dot(out_grads, other[:rows_r], 1 - core)
    proj_h = near_h + dot(hidden_acts, other[rows_r:], 1 - core)

    part_g = sum_x(proj_g)
    part_h = sum_x(proj_h)
    full_g = part_g + swap(part_g, "h")
    full_h = part_h + swap(part_h, "h")
    token_score = (full_h * full_g).reshape(share, 2 * QB, RANK).sum(axis=2)

    counts = doc_tokens[0]
    ends = jnp.cumsum(counts)
    starts = ends - counts
    places = jnp.arange(share, dtype=jnp.int32) + at_x * share
    inside = ((places[None, :] >= starts[:, None]) & (places[None, :] < ends[:, None])).astype(
        jnp.float32
    )
    partial = jnp.dot(
        inside, token_score, precision=lax.Precision.HIGHEST, preferred_element_type=jnp.float32
    )
    copies = jnp.broadcast_to(partial[None], (X, *partial.shape))
    summed = lax.all_to_all(copies, "x", 0, 0, tiled=True).sum(axis=0)
    return summed / jnp.sqrt(jnp.float32(RANK * (tok_rows // 4)))


def solution(mesh):
    fine = Mesh(mesh.devices.reshape(Z, Y, C, H, X), ("z", "y", "c", "h", "x"))
    dp, tensor = ("z", "y", "c"), ("h", "x")
    return jax.shard_map(
        shards,
        mesh=fine,
        in_specs=(
            P(dp, tensor),
            P(dp, tensor),
            P(dp, tensor, None),
            P(dp, tensor, None),
            P(dp, None),
            P(),
        ),
        out_specs=P(dp, None),
        check_vma=False,
    )
```

```python
import jax
import jax.numpy as jnp
from jax import lax
from jax.sharding import Mesh
from jax.sharding import PartitionSpec as P

QB = 4
RANK = 32
COLS = QB * RANK
Z, Y, C, H, X = 8, 4, 2, 2, 4


def swap(block, axis):
    return lax.ppermute(block, axis, [(0, 1), (1, 0)])


def cut(block, start, size, axis):
    return lax.dynamic_slice_in_dim(block, start, size, axis, allow_negative_indices=False)


def pick(got, sources):
    return jnp.concatenate([cut(got, source, 1, 0)[0] for source in sources], axis=1)


def scatter_cores(right, left, mine, owners):
    rows_r, rows_l = right.shape[0] // C, left.shape[0] // C
    own = jnp.concatenate([right[:rows_r], left[:rows_l], right[rows_r:], left[rows_l:]], axis=0)
    own = own.reshape(Z * Y * C, -1, COLS)
    got = lax.all_to_all(own, ("c", "z", "y"), 0, 0, tiled=True)
    return pick(got, [(owner & 1) * (Z * Y) + (owner >> 1) for owner in owners])


def scatter_chips(right, left, mine, owners):
    got = lax.all_to_all(mine.reshape(Z * Y, -1, COLS), ("z", "y"), 0, 0, tiled=True)
    return pick(got, [owner >> 1 for owner in owners])


def dot(acts, part, side):
    rows = part.shape[0]
    acts = cut(acts, side * rows, rows, 1)
    return jnp.dot(acts, part, preferred_element_type=jnp.float32)


def sum_x(proj):
    parts = lax.all_to_all(proj, "x", 0, 0, tiled=True)
    return parts.reshape(X, -1, proj.shape[1]).sum(axis=0)


def shards(hidden_acts, out_grads, left_factors, right_factors, doc_tokens, owners):
    tok_rows = hidden_acts.shape[0]
    core, at_x = lax.axis_index("c"), lax.axis_index("x")
    device = lax.axis_index(("z", "y", "c"))
    share = tok_rows // X

    right, left = right_factors[0], left_factors[0]
    rows_r = right.shape[0] // C
    owner = owners[0], owners[1]
    rows_l = left.shape[0] // C
    far_l = swap(cut(left, (1 - core) * rows_l, rows_l, 0), "c")
    far_r = swap(cut(right, (1 - core) * rows_r, rows_r, 0), "c")
    wanted = (owner[0] == device) | (owner[1] == device)
    near_r, near_l = cut(right, core * rows_r, rows_r, 0), cut(left, core * rows_l, rows_l, 0)
    mine = jnp.concatenate(
        [jnp.where(wanted, near_r, far_r), jnp.where(wanted, near_l, far_l)], axis=0
    )
    picked = lax.cond(
        owner[0] ^ owner[1] == 1, scatter_cores, scatter_chips, right, left, mine, owner
    )

    copies = jnp.broadcast_to(picked[None], (Z * Y, *picked.shape))
    mine = lax.all_to_all(copies, ("z", "y"), 0, 0, tiled=True).reshape(-1, 2 * COLS)
    other = swap(mine, "c")

    near_g = dot(out_grads, mine[:rows_r], core)
    near_h = dot(hidden_acts, mine[rows_r:], core)
    proj_g = near_g + dot(out_grads, other[:rows_r], 1 - core)
    proj_h = near_h + dot(hidden_acts, other[rows_r:], 1 - core)

    part_g = sum_x(proj_g)
    part_h = sum_x(proj_h)
    full_g = part_g + swap(part_g, "h")
    full_h = part_h + swap(part_h, "h")
    token_score = (full_h * full_g).reshape(share, 2 * QB, RANK).sum(axis=2)

    counts = doc_tokens[0]
    ends = jnp.cumsum(counts)
    starts = ends - counts
    places = jnp.arange(share, dtype=jnp.int32) + at_x * share
    inside = ((places[None, :] >= starts[:, None]) & (places[None, :] < ends[:, None])).astype(
        jnp.float32
    )
    partial = jnp.dot(
        inside, token_score, precision=lax.Precision.HIGHEST, preferred_element_type=jnp.float32
    )
    copies = jnp.broadcast_to(partial[None], (X, *partial.shape))
    summed = lax.all_to_all(copies, "x", 0, 0, tiled=True).sum(axis=0)
    return summed / jnp.sqrt(jnp.float32(RANK * (tok_rows // 4)))


def solution(mesh):
    fine = Mesh(mesh.devices.reshape(Z, Y, C, H, X), ("z", "y", "c", "h", "x"))
    dp, tensor = ("z", "y", "c"), ("h", "x")
    return jax.shard_map(
        shards,
        mesh=fine,
        in_specs=(
            P(dp, tensor),
            P(dp, tensor),
            P(dp, tensor, None),
            P(dp, tensor, None),
            P(dp, None),
            P(),
        ),
        out_specs=P(dp, None),
        check_vma=False,
    )
```
